256 devices in a mesh: ctx: 64 (over y, z, core), head: 4 (over x).
Axes of the slice: x: 4, y: 4, z: 8, core: 2. Of those that a mesh axis runs over, the one named last changes fastest.
Arguments:
- queries: bfloat16 [16384, 4096], P(('ctx', 'head')), may hold values from -9 to 9
- keys: bfloat16 [16384, 1024], P(('ctx', 'head')), may hold values from -9 to 9
- values: bfloat16 [16384, 1024], P(('ctx', 'head')), may hold values from -6 to 6
- output_cotangent: bfloat16 [16384, 4096], P(('ctx', 'head')), may hold values from -6 to 6
- tile_order: int32 [256], P('ctx'), may hold values from 0 to 255, each once
- doc_lengths: int32 [4], replicated, may hold values from 1 to 8192, 16384 in all
- read_peer: int32 [4096, 1], replicated, may hold values from 0 to 63; in each aligned block of 64 rows (0 to 63, 64 to 127, ...) at most 2 rows name the same one
- read_slot: int32 [4096], replicated, may hold values from 0 to 3
Outputs:
- attended: bfloat16 [16384, 4096], P(('ctx', 'head'))
- grad_queries: bfloat16 [16384, 4096], P(('ctx', 'head'))
- grad_keys: bfloat16 [16384, 1024], P(('ctx', 'head'))
- grad_values: bfloat16 [16384, 1024], P(('ctx', 'head'))
The draws below stay inside these ranges and needn't reach their ends.
Inputs may be any that keep to these rules, and one draw needn't show every extreme that they name: `read_peer`: the 64 rows of one group (an aligned block) name any one group at most 2 times; some block names some group exactly 2 times.
All inputs are finite; a program needn't handle non-finite values.
Results may differ from the reference program's by a relative error of at most 0.028.
Values may be sent and summed in bfloat16 or wider, within the bound.
No kernel may reach another device: no remote copies, remote signals or barrier semaphores. Data moves between devices by JAX's collectives and lax.ppermute only.
A program may use at most 192 MiB of HBM per device.

```python
import math
import jax
import jax.numpy as jnp
import numpy as np
from jax import lax

QUERY_HEADS = 32
KEY_VALUE_HEADS = 8
HEAD_SIZE = 128
TILE = 64
TD = 4
MOST = 2
NDOC = 4
READS = 64
NT = 256
PACKED_TOKENS = 16384
N_CTX = 64


def draw_queries(key, part):
    key = jax.random.fold_in(key, 1)
    return jnp.clip(jax.random.normal(key, (PACKED_TOKENS, QUERY_HEADS * HEAD_SIZE), jnp.float32), -6.0, 6.0).astype(jnp.bfloat16)


def draw_keys(key, part):
    key = jax.random.fold_in(key, 2)
    return jnp.clip(jax.random.normal(key, (PACKED_TOKENS, KEY_VALUE_HEADS * HEAD_SIZE), jnp.float32), -6.0, 6.0).astype(jnp.bfloat16)


def plant(result, stream_key, smallest, largest):
    shape = result.shape
    index_at = [jax.random.randint(jax.random.fold_in(stream_key, axis), (), 0, shape[axis]) for axis in range(len(shape))]
    result = result.at[tuple(index_at)].set(smallest)
    longest = shape.index(max(shape))
    index_at[longest] = (index_at[longest] + 1) % shape[longest]
    return result.at[tuple(index_at)].set(largest)


def levels(stream_key, extent, split, least, largest):
    gain, own = 1.0, jax.random.fold_in(stream_key, 6)
    for axis_at, shards_of in split:
        draws = jnp.exp(jax.random.uniform(jax.random.fold_in(own, axis_at), (shards_of,), jnp.float32, least / len(split), largest / len(split)))
        gain = gain * jnp.repeat(draws, extent[axis_at] // shards_of).reshape([-1 if axis == axis_at else 1 for axis in range(len(extent))])
    return gain


def profile(amount, total, bound, lean):
    weights = [(1 << 20) // math.isqrt(grade ** lean) + 1 for grade in range(2, amount + 1)]
    surplus, holding = total - bound - (amount - 1), [1] * (amount - 1)
    while surplus > 0:
        candidates = [i for i in range(amount - 1) if holding[i] < bound]
        pool, remaining = sum([weights[i] for i in candidates]), surplus
        for i in candidates:
            more = min(bound - holding[i], max(1, remaining * weights[i] // pool), surplus)
            holding[i] = holding[i] + more
            surplus = surplus - more
    return np.array([bound] + holding)


def uneven_parts(stream_key, number_of, total, limit, skew):
    if number_of == 2:
        one = jax.random.randint(stream_key, (), max(1, total - limit), min(limit, total - 1) + 1)
        return jnp.stack([one, total - one])
    sizes = jnp.asarray(profile(number_of, total, limit, skew), jnp.int32)
    twos = (number_of - 1) // 2
    donor, sink = sizes[1:1 + 2 * twos:2], sizes[2:2 + 2 * twos:2]
    slack = jnp.minimum(donor - 1, limit - sink)
    passed = jax.random.randint(jax.random.fold_in(stream_key, 1), (twos,), 0, 1 << 20) % (slack + 1)
    sizes = sizes.at[1:1 + 2 * twos:2].set(donor - passed).at[2:2 + 2 * twos:2].set(sink + passed)
    return sizes[jax.random.permutation(jax.random.fold_in(stream_key, 2), number_of)]


def shared_out(key, own, number, rows, count, top, most, lean):
    ranking = jax.random.permutation(key, count)
    crowded, usual = load_shares(count, rows * top, most, lean, True), load_shares(count, rows * top, most, lean, False)
    places = jnp.arange(count)

    def named(sizes, offset_by):
        used = int((sizes > 0).sum())
        fixed = max(1, used // 4)
        passed = fixed + (places - fixed + offset_by * (used - fixed)) % max(1, count - fixed)
        return jnp.zeros((count,), jnp.int32).at[ranking[jnp.where(places < fixed, places, passed)]].set(jnp.asarray(sizes, jnp.int32))

    sizes = jnp.where(number % 4 == 0, named(crowded, number // 4), named(usual, number - number // 4 - 1))
    mixed = jax.random.permutation(jax.random.fold_in(own, 3), count)
    giver, sink = mixed[0:count // 2 * 2:2], mixed[1:count // 2 * 2:2]
    margin = jnp.minimum(sizes[giver] - 1, most - sizes[sink]) // 2
    margin = jnp.where((giver == ranking[0]) | (sink == ranking[0]) | (sizes[sink] == 0), 0, jnp.maximum(margin, 0))
    passed = jax.random.randint(jax.random.fold_in(own, 4), (count // 2,), 0, 1 << 20) % (margin + 1)
    sizes = sizes.at[giver].add(-passed).at[sink].add(passed)
    members = jnp.searchsorted(jnp.cumsum(sizes), jnp.arange(rows * top), side="right").astype(jnp.int32)
    listing = members.reshape(top, rows).T
    listing = listing[jax.random.permutation(jax.random.fold_in(own, 1), rows)]
    offset_by = jax.random.randint(jax.random.fold_in(own, 2), (rows, 1), 0, top)
    return jnp.take_along_axis(listing, (jnp.arange(top)[None, :] + offset_by) % top, axis=1)


def load_shares(amount, total, reach, lean, full):
    portions = [(1 << 20) // math.isqrt(grade ** lean) + 1 for grade in range(1, amount + 1)]
    largest = reach if full else min(reach, max(-(-total // amount), total * portions[0] // sum(portions)))
    least = 1 if total - largest >= amount - 1 else 0
    counts, rest = [largest] + [least] * (amount - 1), total - largest - least * (amount - 1)
    while rest > 0:
        candidates = [i for i in range(1, amount) if counts[i] < largest] or [i for i in range(1, amount) if counts[i] < reach]
        mass, left = sum([portions[i] for i in candidates]), rest
        for i in candidates:
            more = min(reach - counts[i], max(1, left * portions[i] // mass), rest)
            counts[i] = counts[i] + more
            rest = rest - more
    return np.array(counts)


def gaussian(key, extent, width, limit, split=(), held_as=jnp.bfloat16):
    factor_of = levels(key, extent, split, -0.22, 0.18) if split else 1.0
    drawn = jax.random.normal(key, extent, jnp.float32) * width * factor_of
    return jnp.minimum(jnp.maximum(drawn, -limit), limit).astype(held_as)


def setup_inputs(seed: int = 0) -> dict:
    streams_of = jax.random.split(jax.random.key(seed), 9)
    queries = draw_queries(jax.random.fold_in(streams_of[8], 71), 0)
    keys = draw_keys(jax.random.fold_in(streams_of[8], 71), 0)
    values = gaussian(streams_of[2], (PACKED_TOKENS, KEY_VALUE_HEADS * HEAD_SIZE), 1.0, 6.0, ((0, 256),))
    output_cotangent = gaussian(streams_of[3], (PACKED_TOKENS, QUERY_HEADS * HEAD_SIZE), 1.0, 6.0, ((0, 256),))
    tile_order = jax.random.permutation(streams_of[4], NT).astype(jnp.int32)
    doc_lengths = uneven_parts(streams_of[5], NDOC, PACKED_TOKENS, PACKED_TOKENS // 2, 2).astype(jnp.int32)
    read_peer_keys = jax.random.split(jax.random.fold_in(streams_of[6], 1), (N_CTX * READS) // READS)
    read_peer_turns = jax.random.permutation(jax.random.fold_in(streams_of[6], 3), (N_CTX * READS) // READS)
    read_peer = jax.vmap(lambda own, number: shared_out(jax.random.fold_in(streams_of[6], 2), own, number, READS, N_CTX, 1, MOST, 2))(read_peer_keys, read_peer_turns).reshape((N_CTX * READS, 1))
    read_slot = plant(jax.random.randint(streams_of[7], (N_CTX * READS,), 0, TD), jax.random.fold_in(streams_of[7], 1), 0, TD - 1).astype(jnp.int32)
    return dict(queries=queries, keys=keys, values=values, output_cotangent=output_cotangent, tile_order=tile_order, doc_lengths=doc_lengths, read_peer=read_peer, read_slot=read_slot)


def read_table(peer_column, slot_column, groups, read_count, tiles_each):
    peer_rows = peer_column.reshape(groups, read_count)
    base_rows = slot_column.reshape(groups, read_count)
    entry_ids = jnp.arange(read_count, dtype=jnp.int32)
    same_peer = peer_rows[:, :, None] == peer_rows[:, None, :]
    earlier = entry_ids[None, None, :] < entry_ids[None, :, None]
    occurrence = jnp.sum((same_peer & earlier).astype(jnp.int32), axis=2).astype(jnp.int32)
    first_entry = jnp.min(jnp.where(same_peer, entry_ids[None, None, :], read_count), axis=2).astype(jnp.int32)
    first_base = jnp.take_along_axis(base_rows, first_entry, axis=1)
    return peer_rows, occurrence, ((first_base + occurrence) % tiles_each).astype(jnp.int32)


def document_of(positions, doc_lengths):
    doc_ends = jnp.cumsum(doc_lengths, dtype=jnp.int32)
    return jnp.sum((positions[..., None] >= doc_ends).astype(jnp.int32), axis=-1).astype(jnp.int32)


def rounded_copy(array):
    return lax.optimization_barrier(array.astype(jnp.bfloat16)).astype(jnp.float32)


def reference(queries, keys, values, output_cotangent, tile_order, doc_lengths, read_peer, read_slot):
    count_of_rows = TD * TILE
    group_width = QUERY_HEADS // KEY_VALUE_HEADS
    key_value_width = KEY_VALUE_HEADS * HEAD_SIZE
    score_scale = HEAD_SIZE ** -0.5
    peer_rows, occurrence, slot_ids = read_table(read_peer[:, 0], read_slot, N_CTX, READS, TD)
    within = jnp.arange(TILE, dtype=jnp.int32)
    token_pos = (tile_order[:, None] * TILE + within[None, :]).reshape(PACKED_TOKENS).astype(jnp.int32)
    token_doc = document_of(token_pos, doc_lengths)

    def one_group(carry, group):
        own_row_slice = (group * count_of_rows + jnp.arange(count_of_rows, dtype=jnp.int32)).astype(jnp.int32)
        group_peers = peer_rows[group]
        usable = group_peers != group
        read_rows = ((group_peers * TD + slot_ids[group])[:, None] * TILE + within[None, :]).reshape(-1).astype(jnp.int32)
        key_row_slice = jnp.concatenate([own_row_slice, read_rows])
        key_ok = jnp.concatenate([jnp.ones((count_of_rows,), jnp.bool_), jnp.repeat(usable, TILE)])
        same_doc = token_doc[key_row_slice][None, :] == token_doc[own_row_slice][:, None]
        causal = token_pos[key_row_slice][None, :] <= token_pos[own_row_slice][:, None]
        allowed = key_ok[None, :] & same_doc & causal
        query_tile_block = queries[own_row_slice].astype(jnp.float32).reshape(count_of_rows, KEY_VALUE_HEADS, group_width, HEAD_SIZE)
        gradient_block = output_cotangent[own_row_slice].astype(jnp.float32).reshape(count_of_rows, KEY_VALUE_HEADS, group_width, HEAD_SIZE)
        key_tile_block = keys[key_row_slice].astype(jnp.float32).reshape(-1, KEY_VALUE_HEADS, HEAD_SIZE)
        value_tile_block = values[key_row_slice].astype(jnp.float32).reshape(-1, KEY_VALUE_HEADS, HEAD_SIZE)
        scores = jnp.einsum("qgjd,kgd->gjqk", query_tile_block, key_tile_block) * score_scale
        scores = jnp.where(allowed, scores, -jnp.inf)
        shifted = jnp.exp(scores - jnp.max(scores, axis=3, keepdims=True))
        probability = shifted / jnp.sum(shifted, axis=3, keepdims=True)
        rounded = rounded_copy(probability)
        output = rounded_copy(jnp.einsum("gjqk,kgd->qgjd", rounded, value_tile_block))
        row_delta = jnp.transpose(jnp.sum(gradient_block * output, axis=3), (1, 2, 0))
        dprobs = jnp.einsum("qgjd,kgd->gjqk", gradient_block, value_tile_block)
        dscores = rounded_copy(probability * (dprobs - row_delta[..., None]))
        grad_q = jnp.einsum("gjqk,kgd->qgjd", dscores, key_tile_block) * score_scale
        grad_k = (jnp.einsum("gjqk,qgjd->kgd", dscores, query_tile_block) * score_scale).reshape(-1, key_value_width)
        grad_v = jnp.einsum("gjqk,qgjd->kgd", rounded, gradient_block).reshape(-1, key_value_width)
        terms = jnp.concatenate([grad_k, grad_v], axis=1)
        read_terms = rounded_copy(jnp.where(jnp.repeat(usable, TILE)[:, None], terms[count_of_rows:], 0.0))
        carry = carry.at[own_row_slice].add(terms[:count_of_rows])
        carry = carry.at[read_rows].add(read_terms)
        return carry, (output.reshape(count_of_rows, QUERY_HEADS * HEAD_SIZE).astype(jnp.bfloat16), grad_q.reshape(count_of_rows, QUERY_HEADS * HEAD_SIZE).astype(jnp.bfloat16))

    totals, stacked = lax.scan(one_group, jnp.zeros((PACKED_TOKENS, 2 * key_value_width), jnp.float32), jnp.arange(N_CTX, dtype=jnp.int32))
    attended = stacked[0].reshape(PACKED_TOKENS, QUERY_HEADS * HEAD_SIZE)
    grad_queries = stacked[1].reshape(PACKED_TOKENS, QUERY_HEADS * HEAD_SIZE)
    return attended, grad_queries, totals[:, :key_value_width].astype(jnp.bfloat16), totals[:, key_value_width:].astype(jnp.bfloat16)
```

```python
import jax
import jax.numpy as jnp
from jax import lax
from jax.experimental import pallas as pl
from jax.experimental.pallas import tpu as pltpu
from jax.sharding import Mesh, PartitionSpec as P

HEAD = 128
TILE = 64
SLOTS = 4
KV_HEADS = 8
REP = 4
NX, NY, NZ, NC = 4, 4, 8, 2
GROUPS = NY * NZ * NC
TILES = GROUPS * SLOTS
READS = 64
CHUNK = 4
MOST_TILES = 68
MOST_CHUNKS = MOST_TILES // CHUNK
ROWS = REP * TILE
SCALE = HEAD ** -0.5
LOG2E = 1.4426950408889634
AXES = ("y", "z", "core", "x")
NEG = -1e30


def plan(tile_order, doc_lengths, read_peer, read_slot):
    x, y, core = lax.axis_index("x"), lax.axis_index("y"), lax.axis_index("core")
    ends = jnp.cumsum(doc_lengths, dtype=jnp.int32)

    def mine(table):
        table = table.reshape(NY, NZ, NC, READS)
        table = lax.dynamic_index_in_dim(table, y, 0, keepdims=False)
        return lax.dynamic_index_in_dim(table, core, 1, keepdims=False)

    peers, bases = mine(read_peer), mine(read_slot)
    group = (y * NZ + jnp.arange(NZ, dtype=jnp.int32)) * NC + core
    all_groups = jnp.arange(GROUPS, dtype=jnp.int32)
    same = peers[:, :, None] == all_groups[None, None, :]
    count = jnp.sum(same.astype(jnp.int32), axis=1)
    entry = jnp.arange(READS, dtype=jnp.int32)
    first = jnp.min(jnp.where(same, (entry[None, :] * SLOTS + bases)[:, :, None], READS * SLOTS), axis=1)
    slot = jnp.arange(SLOTS, dtype=jnp.int32)
    listed = ((slot[None, None, :] - first[:, :, None]) & (SLOTS - 1)) < count[:, :, None]
    listed = listed | (all_groups[None, :] == group[:, None])[:, :, None]
    listed = listed.reshape(NZ, TILES)
    order = tile_order.reshape(NY, NZ, NC, SLOTS)
    own = lax.dynamic_index_in_dim(order, y, 0, keepdims=False)
    own = lax.dynamic_index_in_dim(own, core, 1, keepdims=False)
    own = lax.dynamic_index_in_dim(own, x, 1, keepdims=False)
    start = jnp.max(jnp.where(ends[None, :] <= own[:, None] * TILE, ends[None, :], 0), axis=1)
    need = (
        listed
        & (tile_order[None, :] <= own[:, None])
        & (tile_order[None, :] * TILE + (TILE - 1) >= start[:, None])
    )
    rank = jnp.cumsum(need.astype(jnp.int32), axis=1)
    t = jnp.arange(TILES, dtype=jnp.int32)
    tx, tc, tz, ty = t % 4, (t // 4) % 2, (t // 8) % 8, t // 64
    place = ((tx * NY + ty) * NC + tc) * NZ + tz
    code = place + TILES * (tile_order + 1)
    wanted = jnp.where(need, rank, 0)[:, :, None] == 1 + jnp.arange(MOST_TILES, dtype=jnp.int32)
    codes = jnp.sum(jnp.where(wanted, code[None, :, None], 0), axis=1)
    return codes, rank[:, -1], own, ends


def attend(codes, counts, own, ends, q_ref, g_ref, kv_ref, o_ref, dq_ref, dkv_ref, acc, st):
    acc[...] = jnp.zeros_like(acc)
    key_at = lax.broadcasted_iota(jnp.int32, (TILE, ROWS), 0)
    lane = lax.broadcasted_iota(jnp.int32, (1, ROWS), 1) & (TILE - 1)

    def stacked(ref, s):
        return jnp.concatenate([ref[s, :, h * HEAD:(h + 1) * HEAD] for h in range(REP)], axis=0)

    def one_tile(s, carry):
        q = stacked(q_ref, s)
        g = stacked(g_ref, s)
        q_pos = own[s] * TILE + lane
        low = jnp.zeros_like(q_pos)
        for k in range(4):
            low = jnp.where(q_pos >= ends[k], ends[k], low)
        chunks = (counts[s] + (CHUNK - 1)) // CHUNK

        def places(c):
            return [codes[s, c * CHUNK + j] for j in range(CHUNK)]

        def scores(c, top):
            found = places(c)
            keys = jnp.concatenate([kv_ref[f & (TILES - 1), :, :HEAD] for f in found], axis=0)
            raw = lax.dot_general(keys, q, (((1,), (1,)), ((), ())), preferred_element_type=jnp.float32)
            for j, f in enumerate(found):
                base = (f // TILES - 1) * TILE
                part = raw[j * TILE:(j + 1) * TILE]
                part = jnp.where((key_at <= q_pos - base) & (key_at >= low - base), part, NEG)
                st[c, j * TILE:(j + 1) * TILE, :] = part
                top = jnp.maximum(top, jnp.max(part.reshape(TILE // 8, 8, ROWS), axis=0))
            return top

        top = lax.fori_loop(0, chunks, scores, jnp.full((8, ROWS), NEG, jnp.float32))
        top = jnp.max(top, axis=0, keepdims=True) * (SCALE * LOG2E)

        def forward(c, held):
            total, out = held
            prob = jnp.exp2(st[c] * (SCALE * LOG2E) - top)
            st[c] = prob
            total = total + jnp.sum(prob.reshape(CHUNK * TILE // 8, 8, ROWS), axis=0)
            vals = jnp.concatenate([kv_ref[f & (TILES - 1), :, HEAD:] for f in places(c)], axis=0)
            out = out + lax.dot_general(
                vals, prob.astype(jnp.bfloat16), (((0,), (0,)), ((), ())),
                preferred_element_type=jnp.float32)
            return total, out

        total, out = lax.fori_loop(
            0, chunks, forward,
            (jnp.zeros((8, ROWS), jnp.float32), jnp.zeros((HEAD, ROWS), jnp.float32)))
        inv = 1.0 / jnp.sum(total, axis=0, keepdims=True)
        out = (out * inv).astype(jnp.bfloat16).astype(jnp.float32)
        delta = jnp.sum(out * g.astype(jnp.float32).T, axis=0, keepdims=True)
        out = out.T.astype(jnp.bfloat16)
        for h in range(REP):
            o_ref[s, :, h * HEAD:(h + 1) * HEAD] = out[h * TILE:(h + 1) * TILE]

        def backward(c, dq):
            found = places(c)
            prob = st[c] * inv
            keys = jnp.concatenate([kv_ref[f & (TILES - 1), :, :HEAD] for f in found], axis=0)
            vals = jnp.concatenate([kv_ref[f & (TILES - 1), :, HEAD:] for f in found], axis=0)
            dprob = lax.dot_general(vals, g, (((1,), (1,)), ((), ())), preferred_element_type=jnp.float32)
            dscore = (prob * (dprob - delta)).astype(jnp.bfloat16)
            dq = dq + lax.dot_general(
                keys, dscore, (((0,), (0,)), ((), ())), preferred_element_type=jnp.float32)
            dk = jnp.dot(dscore, q, preferred_element_type=jnp.float32)
            dv = jnp.dot(prob.astype(jnp.bfloat16), g, preferred_element_type=jnp.float32)
            for j, f in enumerate(found):
                at = f & (TILES - 1)
                acc[at, :, :HEAD] += dk[j * TILE:(j + 1) * TILE]
                acc[at, :, HEAD:] += dv[j * TILE:(j + 1) * TILE]
            return dq

        dq = lax.fori_loop(0, chunks, backward, jnp.zeros((HEAD, ROWS), jnp.float32))
        dq = (dq * SCALE).T.astype(jnp.bfloat16)
        for h in range(REP):
            dq_ref[s, :, h * HEAD:(h + 1) * HEAD] = dq[h * TILE:(h + 1) * TILE]
        return carry

    lax.fori_loop(0, NZ, one_tile, 0)

    def finish(i, carry):
        dkv_ref[i, :, :HEAD] = (acc[i, :, :HEAD] * SCALE).astype(jnp.bfloat16)
        dkv_ref[i, :, HEAD:] = acc[i, :, HEAD:].astype(jnp.bfloat16)
        return carry

    lax.fori_loop(0, TILES, finish, 0, unroll=4)


def attention(codes, counts, own, ends, q, g, kv):
    smem = pl.BlockSpec(memory_space=pltpu.SMEM)
    vmem = pl.BlockSpec(memory_space=pltpu.VMEM)
    wide = jax.ShapeDtypeStruct((NZ, TILE, REP * HEAD), jnp.bfloat16)
    return pl.pallas_call(
        attend,
        out_shape=(wide, wide, jax.ShapeDtypeStruct((TILES, TILE, 2 * HEAD), jnp.bfloat16)),
        in_specs=[smem] * 4 + [vmem] * 3,
        out_specs=(vmem, vmem, vmem),
        scratch_shapes=[
            pltpu.VMEM((TILES, TILE, 2 * HEAD), jnp.float32),
            pltpu.VMEM((MOST_CHUNKS, CHUNK * TILE, ROWS), jnp.float32),
        ],
        compiler_params=pltpu.CompilerParams(vmem_limit_bytes=56 * 1024 * 1024),
        name="attend",
    )(codes, counts, own, ends, q, g, kv)


def exchange(blocks, axes):
    return lax.all_to_all(blocks, axes, split_axis=0, concat_axis=0, tiled=True)


def per_device(queries, keys, values, output_cotangent, tile_order, doc_lengths, read_peer, read_slot):
    order = lax.all_gather(tile_order, ("y", "z", "core"), axis=0, tiled=True)
    codes, counts, own, ends = plan(order, doc_lengths, read_peer[:, 0], read_slot)
    kv = jnp.concatenate(
        [keys.reshape(TILE, KV_HEADS, HEAD), values.reshape(TILE, KV_HEADS, HEAD)], axis=2)
    kv = exchange(kv.transpose(1, 0, 2), "z")
    kv = lax.all_gather(kv, ("x", "y", "core"), axis=0, tiled=True)
    q = exchange(queries.reshape(TILE, KV_HEADS, REP * HEAD).transpose(1, 0, 2), "z")
    g = exchange(output_cotangent.reshape(TILE, KV_HEADS, REP * HEAD).transpose(1, 0, 2), "z")
    out, dq, dkv = attention(codes, counts, own, ends, q, g, kv)
    dkv = exchange(dkv.reshape(NX * NY * NC, NZ * TILE, 2 * HEAD), ("x", "y", "core"))
    dkv = jnp.sum(dkv.astype(jnp.float32), axis=0).astype(jnp.bfloat16)
    dkv = exchange(dkv.reshape(NZ, TILE, 2 * HEAD), "z").transpose(1, 0, 2)
    out = exchange(out, "z").transpose(1, 0, 2).reshape(TILE, KV_HEADS * REP * HEAD)
    dq = exchange(dq, "z").transpose(1, 0, 2).reshape(TILE, KV_HEADS * REP * HEAD)
    return (
        out,
        dq,
        dkv[:, :, :HEAD].reshape(TILE, KV_HEADS * HEAD),
        dkv[:, :, HEAD:].reshape(TILE, KV_HEADS * HEAD),
    )


def solution(mesh):
    fine = Mesh(mesh.devices.reshape(NY, NZ, NC, NX), AXES)
    rows = P(AXES, None)
    return jax.shard_map(
        per_device,
        mesh=fine,
        in_specs=(rows, rows, rows, rows, P(("y", "z", "core")), P(), P(), P()),
        out_specs=(rows, rows, rows, rows),
        check_vma=False,
    )
```

```python
import jax
import jax.numpy as jnp
from jax import lax
from jax.experimental import pallas as pl
from jax.experimental.pallas import tpu as pltpu
from jax.sharding import Mesh, PartitionSpec as P

HEAD = 128
TILE = 64
SLOTS = 4
KV_HEADS = 8
REP = 4
NX, NY, NZ, NC = 4, 4, 8, 2
GROUPS = NY * NZ * NC
TILES = GROUPS * SLOTS
READS = 64
CHUNK = 4
MOST_TILES = 68
MOST_CHUNKS = MOST_TILES // CHUNK
ROWS = REP * TILE
SCALE = HEAD ** -0.5
LOG2E = 1.4426950408889634
AXES = ("y", "z", "core", "x")
NEG = -1e30


def plan(tile_order, doc_lengths, read_peer, read_slot):
    x, y, core = lax.axis_index("x"), lax.axis_index("y"), lax.axis_index("core")
    ends = jnp.cumsum(doc_lengths, dtype=jnp.int32)

    def mine(table):
        table = table.reshape(NY, NZ, NC, READS)
        table = lax.dynamic_index_in_dim(table, y, 0, keepdims=False)
        return lax.dynamic_index_in_dim(table, core, 1, keepdims=False)

    peers, bases = mine(read_peer), mine(read_slot)
    group = (y * NZ + jnp.arange(NZ, dtype=jnp.int32)) * NC + core
    all_groups = jnp.arange(GROUPS, dtype=jnp.int32)
    same = peers[:, :, None] == all_groups[None, None, :]
    count = jnp.sum(same.astype(jnp.int32), axis=1)
    entry = jnp.arange(READS, dtype=jnp.int32)
    first = jnp.min(jnp.where(same, (entry[None, :] * SLOTS + bases)[:, :, None], READS * SLOTS), axis=1)
    slot = jnp.arange(SLOTS, dtype=jnp.int32)
    listed = ((slot[None, None, :] - first[:, :, None]) & (SLOTS - 1)) < count[:, :, None]
    listed = listed | (all_groups[None, :] == group[:, None])[:, :, None]
    listed = listed.reshape(NZ, TILES)
    order = tile_order.reshape(NY, NZ, NC, SLOTS)
    own = lax.dynamic_index_in_dim(order, y, 0, keepdims=False)
    own = lax.dynamic_index_in_dim(own, core, 1, keepdims=False)
    own = lax.dynamic_index_in_dim(own, x, 1, keepdims=False)
    start = jnp.max(jnp.where(ends[None, :] <= own[:, None] * TILE, ends[None, :], 0), axis=1)
    need = (
        listed
        & (tile_order[None, :] <= own[:, None])
        & (tile_order[None, :] * TILE + (TILE - 1) >= start[:, None])
    )
    rank = jnp.cumsum(need.astype(jnp.int32), axis=1)
    t = jnp.arange(TILES, dtype=jnp.int32)
    tx, tc, tz, ty = t % 4, (t // 4) % 2, (t // 8) % 8, t // 64
    place = ((tx * NY + ty) * NC + tc) * NZ + tz
    dx, dy, half = (tx - x) & 3, (ty - y) & 3, tz // 4
    hops, hops2 = jnp.where(half == 0, dx, dy), jnp.where(half == 0, dy, dx)
    goal = ((((tc ^ core) * 2 + half) * 4 + hops) * 2 + (tz // 2) % 2) * 8 + hops2 * 2 + tz % 2
    code = place + TILES * goal + TILES * TILES * (tile_order + 1)
    wanted = jnp.where(need, rank, 0)[:, :, None] == 1 + jnp.arange(MOST_TILES, dtype=jnp.int32)
    codes = jnp.sum(jnp.where(wanted, code[None, :, None], 0), axis=1)
    return codes, rank[:, -1], own, ends


def attend(codes, counts, own, ends, q_ref, g_ref, kv_ref, o_ref, dq_ref, near_ref, far_ref, acc, st):
    acc[...] = jnp.zeros_like(acc)
    key_at = lax.broadcasted_iota(jnp.int32, (TILE, ROWS), 0)
    lane = lax.broadcasted_iota(jnp.int32, (1, ROWS), 1) & (TILE - 1)

    def stacked(ref, s):
        return jnp.concatenate([ref[s, :, h * HEAD:(h + 1) * HEAD] for h in range(REP)], axis=0)

    def one_tile(s, carry):
        q = stacked(q_ref, s)
        g = stacked(g_ref, s)
        q_pos = own[s] * TILE + lane
        low = jnp.zeros_like(q_pos)
        for k in range(4):
            low = jnp.where(q_pos >= ends[k], ends[k], low)
        chunks = (counts[s] + (CHUNK - 1)) // CHUNK

        def places(c):
            return [codes[s, c * CHUNK + j] for j in range(CHUNK)]

        def scores(c, top):
            found = places(c)
            keys = jnp.concatenate([kv_ref[f & (TILES - 1), :, :HEAD] for f in found], axis=0)
            raw = lax.dot_general(keys, q, (((1,), (1,)), ((), ())), preferred_element_type=jnp.float32)
            for j, f in enumerate(found):
                base = (f // (TILES * TILES) - 1) * TILE
                part = raw[j * TILE:(j + 1) * TILE]
                part = jnp.where((key_at <= q_pos - base) & (key_at >= low - base), part, NEG)
                st[c, j * TILE:(j + 1) * TILE, :] = part
                top = jnp.maximum(top, jnp.max(part.reshape(TILE // 8, 8, ROWS), axis=0))
            return top

        top = lax.fori_loop(0, chunks, scores, jnp.full((8, ROWS), NEG, jnp.float32))
        top = jnp.max(top, axis=0, keepdims=True) * (SCALE * LOG2E)

        def forward(c, held):
            total, out = held
            prob = jnp.exp2(st[c] * (SCALE * LOG2E) - top)
            st[c] = prob
            total = total + jnp.sum(prob.reshape(CHUNK * TILE // 8, 8, ROWS), axis=0)
            vals = jnp.concatenate([kv_ref[f & (TILES - 1), :, HEAD:] for f in places(c)], axis=0)
            out = out + lax.dot_general(
                vals, prob.astype(jnp.bfloat16), (((0,), (0,)), ((), ())),
                preferred_element_type=jnp.float32)
            return total, out

        total, out = lax.fori_loop(
            0, chunks, forward,
            (jnp.zeros((8, ROWS), jnp.float32), jnp.zeros((HEAD, ROWS), jnp.float32)))
        inv = 1.0 / jnp.sum(total, axis=0, keepdims=True)
        out = (out * inv).astype(jnp.bfloat16).astype(jnp.float32)
        delta = jnp.sum(out * g.astype(jnp.float32).T, axis=0, keepdims=True)
        out = out.T.astype(jnp.bfloat16)
        for h in range(REP):
            o_ref[s, :, h * HEAD:(h + 1) * HEAD] = out[h * TILE:(h + 1) * TILE]

        def backward(c, dq):
            found = places(c)
            prob = st[c] * inv
            keys = jnp.concatenate([kv_ref[f & (TILES - 1), :, :HEAD] for f in found], axis=0)
            vals = jnp.concatenate([kv_ref[f & (TILES - 1), :, HEAD:] for f in found], axis=0)
            dprob = lax.dot_general(vals, g, (((1,), (1,)), ((), ())), preferred_element_type=jnp.float32)
            dscore = (prob * (dprob - delta)).astype(jnp.bfloat16)
            dq = dq + lax.dot_general(
                keys, dscore, (((0,), (0,)), ((), ())), preferred_element_type=jnp.float32)
            dk = jnp.dot(dscore, q, preferred_element_type=jnp.float32)
            dv = jnp.dot(prob.astype(jnp.bfloat16), g, preferred_element_type=jnp.float32)
            for j, f in enumerate(found):
                at = (f // TILES) & (TILES - 1)
                acc[at, :, :HEAD] += dk[j * TILE:(j + 1) * TILE]
                acc[at, :, HEAD:] += dv[j * TILE:(j + 1) * TILE]
            return dq

        dq = lax.fori_loop(0, chunks, backward, jnp.zeros((HEAD, ROWS), jnp.float32))
        dq = (dq * SCALE).T.astype(jnp.bfloat16)
        for h in range(REP):
            dq_ref[s, :, h * HEAD:(h + 1) * HEAD] = dq[h * TILE:(h + 1) * TILE]
        return carry

    lax.fori_loop(0, NZ, one_tile, 0)

    def finish(i, carry):
        for ref, at in ((near_ref, i), (far_ref, i + TILES // 2)):
            ref[i, :, :HEAD] = (acc[at, :, :HEAD] * SCALE).astype(jnp.bfloat16)
            ref[i, :, HEAD:] = acc[at, :, HEAD:].astype(jnp.bfloat16)
        return carry

    lax.fori_loop(0, TILES // 2, finish, 0, unroll=2)


def attention(codes, counts, own, ends, q, g, kv):
    smem = pl.BlockSpec(memory_space=pltpu.SMEM)
    vmem = pl.BlockSpec(memory_space=pltpu.VMEM)
    wide = jax.ShapeDtypeStruct((NZ, TILE, REP * HEAD), jnp.bfloat16)
    part = jax.ShapeDtypeStruct((TILES // 2, TILE, 2 * HEAD), jnp.bfloat16)
    return pl.pallas_call(
        attend,
        out_shape=(wide, wide, part, part),
        in_specs=[smem] * 4 + [vmem] * 3,
        out_specs=(vmem, vmem, vmem, vmem),
        scratch_shapes=[
            pltpu.VMEM((TILES, TILE, 2 * HEAD), jnp.float32),
            pltpu.VMEM((MOST_CHUNKS, CHUNK * TILE, ROWS), jnp.float32),
        ],
        compiler_params=pltpu.CompilerParams(vmem_limit_bytes=56 * 1024 * 1024),
        name="attend",
    )(codes, counts, own, ends, q, g, kv)


def exchange(blocks, axes):
    return lax.all_to_all(blocks, axes, split_axis=0, concat_axis=0, tiled=True)


def shift(array, axis, by):
    size = lax.axis_size(axis)
    return lax.ppermute(array, axis, [(i, (i + by) % size) for i in range(size)])


def added(*arrays):
    return sum(a.astype(jnp.float32) for a in arrays).astype(jnp.bfloat16)


def summed_at_owner(near, far):
    total = added(near, shift(far, "core", 1))
    ways = (("x", "y"), ("y", "x"))
    sent = []
    for half, (axis, _) in enumerate(ways):
        t = total[half]
        up = shift(jnp.stack([t[2, 0], t[1, 1]]), axis, 1)
        down = shift(jnp.stack([t[2, 1], t[3, 0]]), axis, -1)
        sent.append((up, down))
    passed = []
    for half, (axis, _) in enumerate(ways):
        t, (up, down) = total[half], sent[half]
        passed.append((shift(added(t[1, 0], up[0]), axis, 1), shift(added(t[3, 1], down[0]), axis, -1)))
    rows = []
    for half in range(2):
        t, (up, down), (from_low, from_high) = total[half], sent[half], passed[half]
        rows.append(jnp.stack([added(t[0, 0], from_low, down[1]), added(t[0, 1], from_high, up[1])]))
    parts = []
    for (_, axis), row in zip(ways, rows):
        parts.append(added(
            row[:, 0], shift(row[:, 1], axis, 1), shift(row[:, 2], axis, 2), shift(row[:, 3], axis, -1)))
    return jnp.stack(parts).reshape(NZ, TILE, 2 * HEAD)


def per_device(queries, keys, values, output_cotangent, tile_order, doc_lengths, read_peer, read_slot):
    order = lax.all_gather(tile_order, ("y", "z", "core"), axis=0, tiled=True)
    codes, counts, own, ends = plan(order, doc_lengths, read_peer[:, 0], read_slot)
    kv = jnp.concatenate(
        [keys.reshape(TILE, KV_HEADS, HEAD), values.reshape(TILE, KV_HEADS, HEAD)], axis=2)
    kv = exchange(kv.transpose(1, 0, 2), "z")
    kv = lax.all_gather(kv, ("x", "y", "core"), axis=0, tiled=True)
    q = exchange(queries.reshape(TILE, KV_HEADS, REP * HEAD).transpose(1, 0, 2), "z")
    g = exchange(output_cotangent.reshape(TILE, KV_HEADS, REP * HEAD).transpose(1, 0, 2), "z")
    out, dq, near, far = attention(codes, counts, own, ends, q, g, kv)
    pieces = (2, 4, 2, 4, 2, TILE, 2 * HEAD)
    dkv = summed_at_owner(near.reshape(pieces), far.reshape(pieces))
    dkv = exchange(dkv, "z").transpose(1, 0, 2)
    out = exchange(out, "z").transpose(1, 0, 2).reshape(TILE, KV_HEADS * REP * HEAD)
    dq = exchange(dq, "z").transpose(1, 0, 2).reshape(TILE, KV_HEADS * REP * HEAD)
    return (
        out,
        dq,
        dkv[:, :, :HEAD].reshape(TILE, KV_HEADS * HEAD),
        dkv[:, :, HEAD:].reshape(TILE, KV_HEADS * HEAD),
    )


def solution(mesh):
    fine = Mesh(mesh.devices.reshape(NY, NZ, NC, NX), AXES)
    rows = P(AXES, None)
    return jax.shard_map(
        per_device,
        mesh=fine,
        in_specs=(rows, rows, rows, rows, P(("y", "z", "core")), P(), P(), P()),
        out_specs=(rows, rows, rows, rows),
        check_vma=False,
    )
```

```python
import jax
import jax.numpy as jnp
from jax import lax
from jax.experimental import pallas as pl
from jax.experimental.pallas import tpu as pltpu
from jax.sharding import Mesh, PartitionSpec as P

HEAD = 128
TILE = 64
SLOTS = 4
KV_HEADS = 8
REP = 4
NX, NY, NZ, NC = 4, 4, 8, 2
GROUPS = NY * NZ * NC
TILES = GROUPS * SLOTS
READS = 64
CHUNK = 12
MOST_TILES = 72
MOST_CHUNKS = MOST_TILES // CHUNK
ROWS = REP * TILE
WIDE = REP * HEAD
PART = TILES // 4
SCALE = HEAD ** -0.5
LOG2E = 1.4426950408889634
AXES = ("y", "z", "core", "x")
NEG = -1e30


def plan(tile_order, doc_lengths, read_peer, read_slot):
    x, y, core = lax.axis_index("x"), lax.axis_index("y"), lax.axis_index("core")
    ends = jnp.cumsum(doc_lengths, dtype=jnp.int32)

    def mine(table):
        table = table.reshape(NY, NZ, NC, READS)
        table = lax.dynamic_index_in_dim(table, y, 0, keepdims=False)
        return lax.dynamic_index_in_dim(table, core, 1, keepdims=False)

    peers, bases = mine(read_peer), mine(read_slot)
    group = (y * NZ + jnp.arange(NZ, dtype=jnp.int32)) * NC + core
    all_groups = jnp.arange(GROUPS, dtype=jnp.int32)
    same = peers[:, :, None] == all_groups[None, None, :]
    count = jnp.sum(same.astype(jnp.int32), axis=1)
    entry = jnp.arange(READS, dtype=jnp.int32)
    first = jnp.min(jnp.where(same, (entry[None, :] * SLOTS + bases)[:, :, None], READS * SLOTS), axis=1)
    slot = jnp.arange(SLOTS, dtype=jnp.int32)
    listed = ((slot[None, None, :] - first[:, :, None]) & (SLOTS - 1)) < count[:, :, None]
    listed = listed | (all_groups[None, :] == group[:, None])[:, :, None]
    listed = listed.reshape(NZ, TILES)
    order = tile_order.reshape(NY, NZ, NC, SLOTS)
    own = lax.dynamic_index_in_dim(order, y, 0, keepdims=False)
    own = lax.dynamic_index_in_dim(own, core, 1, keepdims=False)
    own = lax.dynamic_index_in_dim(own, x, 1, keepdims=False)
    start = jnp.max(jnp.where(ends[None, :] <= own[:, None] * TILE, ends[None, :], 0), axis=1)
    need = (
        listed
        & (tile_order[None, :] <= own[:, None])
        & (tile_order[None, :] * TILE + (TILE - 1) >= start[:, None])
    )
    rank = jnp.cumsum(need.astype(jnp.int32), axis=1)
    t = jnp.arange(TILES, dtype=jnp.int32)
    tx, tc, tz, ty = t % 4, (t // 4) % 2, (t // 8) % 8, t // 64
    place = ((tx * NY + ty) * NC + tc) * NZ + tz
    dx, dy, half = (tx - x) & 3, (ty - y) & 3, tz // 4
    hops, hops2 = jnp.where(half == 0, dx, dy), jnp.where(half == 0, dy, dx)
    which = hops * 2 + (tz // 2) % 2
    late, piece = jnp.zeros_like(t), jnp.zeros_like(t)
    for case, (stage, at) in enumerate(((1, 0), (1, 1), (1, 2), (0, 1), (0, 0), (0, 2), (0, 3), (1, 3))):
        late, piece = jnp.where(which == case, stage, late), jnp.where(which == case, at, piece)
    goal = ((1 - (tc ^ core)) * 2 + late) * PART + half * 32 + piece * 8 + hops2 * 2 + tz % 2
    code = place + TILES * goal + TILES * TILES * (tile_order + 1)
    wanted = jnp.where(need, rank, 0)[:, :, None] == 1 + jnp.arange(MOST_TILES, dtype=jnp.int32)
    codes = jnp.sum(jnp.where(wanted, code[None, :, None], 0), axis=1)
    return codes, rank[:, -1], own, ends


def attend(codes, counts, own, ends, qg_ref, kv_hbm, od_ref, far1, far2, near1, near2, kv_ref, acc, st, sems):
    load = pltpu.make_async_copy(kv_hbm, kv_ref, sems.at[0])
    load.start()
    acc[...] = jnp.zeros_like(acc)
    load.wait()
    key_at = lax.broadcasted_iota(jnp.int32, (TILE, ROWS), 0)
    lane = lax.broadcasted_iota(jnp.int32, (1, ROWS), 1) & (TILE - 1)

    def stacked(s, start):
        return jnp.concatenate(
            [qg_ref[s, :, start + h * HEAD:start + (h + 1) * HEAD] for h in range(REP)], axis=0)

    def one_tile(s, carry):
        q = stacked(s, 0)
        g = stacked(s, WIDE)
        q_pos = own[s] * TILE + lane
        low = jnp.zeros_like(q_pos)
        for k in range(4):
            low = jnp.where(q_pos >= ends[k], ends[k], low)
        chunks = (counts[s] + (CHUNK - 1)) // CHUNK

        def places(c):
            return [codes[s, c * CHUNK + j] for j in range(CHUNK)]

        def scores(c, top):
            found = places(c)
            keys = jnp.concatenate([kv_ref[f & (TILES - 1), :, :HEAD] for f in found], axis=0)
            raw = lax.dot_general(keys, q, (((1,), (1,)), ((), ())), preferred_element_type=jnp.float32)
            for j, f in enumerate(found):
                base = (f // (TILES * TILES) - 1) * TILE
                part = raw[j * TILE:(j + 1) * TILE]
                part = jnp.where((key_at <= q_pos - base) & (key_at >= low - base), part, NEG)
                st[c, j * TILE:(j + 1) * TILE, :] = part
                top = jnp.maximum(top, jnp.max(part.reshape(TILE // 8, 8, ROWS), axis=0))
            return top

        top = lax.fori_loop(0, chunks, scores, jnp.full((8, ROWS), NEG, jnp.float32))
        top = jnp.max(top, axis=0, keepdims=True) * (SCALE * LOG2E)

        def forward(c, held):
            total, out = held
            prob = jnp.exp2(st[c] * (SCALE * LOG2E) - top)
            st[c] = prob
            total = total + jnp.sum(prob.reshape(CHUNK * TILE // 8, 8, ROWS), axis=0)
            vals = jnp.concatenate([kv_ref[f & (TILES - 1), :, HEAD:] for f in places(c)], axis=0)
            out = out + lax.dot_general(
                vals, prob.astype(jnp.bfloat16), (((0,), (0,)), ((), ())),
                preferred_element_type=jnp.float32)
            return total, out

        total, out = lax.fori_loop(
            0, chunks, forward,
            (jnp.zeros((8, ROWS), jnp.float32), jnp.zeros((HEAD, ROWS), jnp.float32)))
        inv = 1.0 / jnp.sum(total, axis=0, keepdims=True)
        out = (out * inv).astype(jnp.bfloat16).astype(jnp.float32)
        delta = jnp.sum(out * g.astype(jnp.float32).T, axis=0, keepdims=True)
        out = out.T.astype(jnp.bfloat16)
        for h in range(REP):
            od_ref[s, :, h * HEAD:(h + 1) * HEAD] = out[h * TILE:(h + 1) * TILE]

        def backward(c, dq):
            found = places(c)
            prob = st[c] * inv
            keys = jnp.concatenate([kv_ref[f & (TILES - 1), :, :HEAD] for f in found], axis=0)
            vals = jnp.concatenate([kv_ref[f & (TILES - 1), :, HEAD:] for f in found], axis=0)
            dprob = lax.dot_general(vals, g, (((1,), (1,)), ((), ())), preferred_element_type=jnp.float32)
            dscore = (prob * (dprob - delta)).astype(jnp.bfloat16)
            dq = dq + lax.dot_general(
                keys, dscore, (((0,), (0,)), ((), ())), preferred_element_type=jnp.float32)
            dk = jnp.dot(dscore, q, preferred_element_type=jnp.float32) * SCALE
            dv = jnp.dot(prob.astype(jnp.bfloat16), g, preferred_element_type=jnp.float32)
            for j, f in enumerate(found):
                at = (f // TILES) & (TILES - 1)
                acc[at, :, :HEAD] = added(acc[at, :, :HEAD], dk[j * TILE:(j + 1) * TILE])
                acc[at, :, HEAD:] = added(acc[at, :, HEAD:], dv[j * TILE:(j + 1) * TILE])
            return dq

        dq = lax.fori_loop(0, chunks, backward, jnp.zeros((HEAD, ROWS), jnp.float32))
        dq = (dq * SCALE).T.astype(jnp.bfloat16)
        for h in range(REP):
            od_ref[s, :, WIDE + h * HEAD:WIDE + (h + 1) * HEAD] = dq[h * TILE:(h + 1) * TILE]
        return carry

    lax.fori_loop(0, NZ, one_tile, 0)

    stores = [
        pltpu.make_async_copy(acc.at[pl.ds(i * PART, PART)], ref, sems.at[1 + i])
        for i, ref in enumerate((far1, far2, near1, near2))
    ]
    for store in stores:
        store.start()
    for store in stores:
        store.wait()


def attention(codes, counts, own, ends, qg, kv):
    smem = pl.BlockSpec(memory_space=pltpu.SMEM)
    vmem = pl.BlockSpec(memory_space=pltpu.VMEM)
    hbm = pl.BlockSpec(memory_space=pl.ANY)
    part = jax.ShapeDtypeStruct((PART, TILE, 2 * HEAD), jnp.bfloat16)
    return pl.pallas_call(
        attend,
        out_shape=(jax.ShapeDtypeStruct((NZ, TILE, 2 * WIDE), jnp.bfloat16),) + (part,) * 4,
        in_specs=[smem] * 4 + [vmem, hbm],
        out_specs=(vmem,) + (hbm,) * 4,
        scratch_shapes=[
            pltpu.VMEM((TILES, TILE, 2 * HEAD), jnp.bfloat16),
            pltpu.VMEM((TILES, TILE, 2 * HEAD), jnp.bfloat16),
            pltpu.VMEM((MOST_CHUNKS, CHUNK * TILE, ROWS), jnp.float32),
            pltpu.SemaphoreType.DMA((5,)),
        ],
        compiler_params=pltpu.CompilerParams(vmem_limit_bytes=48 * 1024 * 1024),
        name="attend",
    )(codes, counts, own, ends, qg, kv)


def exchange(blocks, axes):
    return lax.all_to_all(blocks, axes, split_axis=0, concat_axis=0, tiled=True)


def shift(array, axis, by):
    size = lax.axis_size(axis)
    return lax.ppermute(array, axis, [(i, (i + by) % size) for i in range(size)])


def added(*arrays):
    return sum(a.astype(jnp.float32) for a in arrays).astype(jnp.bfloat16)


def summed_at_owner(far1, far2, near1, near2):
    first, second = (2, 2, 2, 4, 2, TILE, 2 * HEAD), (2, 4, 4, 2, TILE, 2 * HEAD)
    other1, other2 = shift(far1, "core", 1).reshape(first), shift(far2, "core", 1).reshape(second)
    near1, near2 = near1.reshape(first), near2.reshape(second)
    ways = (("x", "y"), ("y", "x"))
    sent = []
    for half, (axis, _) in enumerate(ways):
        up = added(near1[half, 0], other1[half, 0])
        down = added(near1[half, 1], other1[half, 1])
        sent.append((shift(up, axis, 1), shift(down, axis, -1)))
    passed = []
    for half, (axis, _) in enumerate(ways):
        up, down = sent[half]
        passed.append((
            shift(added(near2[half, 2], other2[half, 2], up[0]), axis, 1),
            shift(added(near2[half, 3], other2[half, 3], down[0]), axis, -1)))
    parts = []
    for half, (_, axis) in enumerate(ways):
        (up, down), (low, high) = sent[half], passed[half]
        row = jnp.stack([
            added(near2[half, 0], other2[half, 0], low, down[1]),
            added(near2[half, 1], other2[half, 1], high, up[1])])
        parts.append(added(
            row[:, 0], shift(row[:, 1], axis, 1), shift(row[:, 2], axis, 2), shift(row[:, 3], axis, -1)))
    return jnp.stack(parts).reshape(NZ, TILE, 2 * HEAD)


def per_device(queries, keys, values, output_cotangent, tile_order, doc_lengths, read_peer, read_slot):
    order = lax.all_gather(tile_order, ("y", "z", "core"), axis=0, tiled=True)
    codes, counts, own, ends = plan(order, doc_lengths, read_peer[:, 0], read_slot)

    def by_head(a, b, width):
        both = [v.reshape(TILE, KV_HEADS, width) for v in (a, b)]
        return exchange(jnp.concatenate(both, axis=2).transpose(1, 0, 2), "z")

    def by_token(blocks, width):
        blocks = exchange(blocks, "z").transpose(1, 0, 2)
        return [blocks[:, :, i * width:(i + 1) * width].reshape(TILE, KV_HEADS * width) for i in range(2)]

    kv = lax.all_gather(by_head(keys, values, HEAD), ("x", "y", "core"), axis=0, tiled=True)
    kv = kv.reshape(TILES, TILE, 2 * HEAD)
    qg = by_head(queries, output_cotangent, WIDE)
    od, *terms = attention(codes, counts, own, ends, qg, kv)
    out, dq = by_token(od, WIDE)
    dk, dv = by_token(summed_at_owner(*terms), HEAD)
    return out, dq, dk, dv


def solution(mesh):
    fine = Mesh(mesh.devices.reshape(NY, NZ, NC, NX), AXES)
    rows = P(AXES, None)
    return jax.shard_map(
        per_device,
        mesh=fine,
        in_specs=(rows, rows, rows, rows, P(("y", "z", "core")), P(), P(), P()),
        out_specs=(rows, rows, rows, rows),
        check_vma=False,
    )
```

```python
import jax
import jax.numpy as jnp
from jax import lax
from jax.experimental import pallas as pl
from jax.experimental.pallas import tpu as pltpu
from jax.sharding import Mesh, PartitionSpec as P

HEAD = 128
TILE = 64
SLOTS = 4
KV_HEADS = 8
REP = 4
NX, NY, NZ, NC = 4, 4, 8, 2
GROUPS = NY * NZ * NC
TILES = GROUPS * SLOTS
READS = 64
CHUNK = 12
MOST_TILES = 72
MOST_CHUNKS = MOST_TILES // CHUNK
ROWS = REP * TILE
WIDE = REP * HEAD
PART = TILES // 8
TOGETHER = 2
SCALE = HEAD ** -0.5
LOG2E = 1.4426950408889634
AXES = ("y", "z", "core", "x")
NEG = -1e30


def plan(tile_order, doc_lengths, read_peer, read_slot):
    x, y, core = lax.axis_index("x"), lax.axis_index("y"), lax.axis_index("core")
    ends = jnp.cumsum(doc_lengths, dtype=jnp.int32)

    def mine(table):
        table = table.reshape(NY, NZ, NC, READS)
        table = lax.dynamic_index_in_dim(table, y, 0, keepdims=False)
        return lax.dynamic_index_in_dim(table, core, 1, keepdims=False)

    peers, bases = mine(read_peer), mine(read_slot)
    group = (y * NZ + jnp.arange(NZ, dtype=jnp.int32)) * NC + core
    all_groups = jnp.arange(GROUPS, dtype=jnp.int32)
    same = peers[:, :, None] == all_groups[None, None, :]
    count = jnp.sum(same.astype(jnp.int32), axis=1)
    entry = jnp.arange(READS, dtype=jnp.int32)
    first = jnp.min(jnp.where(same, (entry[None, :] * SLOTS + bases)[:, :, None], READS * SLOTS), axis=1)
    slot = jnp.arange(SLOTS, dtype=jnp.int32)
    listed = ((slot[None, None, :] - first[:, :, None]) & (SLOTS - 1)) < count[:, :, None]
    listed = listed | (all_groups[None, :] == group[:, None])[:, :, None]
    listed = listed.reshape(NZ, TILES)
    order = tile_order.reshape(NY, NZ, NC, SLOTS)
    own = lax.dynamic_index_in_dim(order, y, 0, keepdims=False)
    own = lax.dynamic_index_in_dim(own, core, 1, keepdims=False)
    own = lax.dynamic_index_in_dim(own, x, 1, keepdims=False)
    start = jnp.max(jnp.where(ends[None, :] <= own[:, None] * TILE, ends[None, :], 0), axis=1)
    need = (
        listed
        & (tile_order[None, :] <= own[:, None])
        & (tile_order[None, :] * TILE + (TILE - 1) >= start[:, None])
    )
    rank = jnp.cumsum(need.astype(jnp.int32), axis=1)
    t = jnp.arange(TILES, dtype=jnp.int32)
    tx, tc, tz, ty = t % 4, (t // 4) % 2, (t // 8) % 8, t // 64
    place = ((tx * NY + ty) * NC + tc) * NZ + tz
    dx, dy, half = (tx - x) & 3, (ty - y) & 3, tz // 4
    hops, hops2 = jnp.where(half == 0, dx, dy), jnp.where(half == 0, dy, dx)
    goal = ((1 - (tc ^ core)) * 4 + hops) * PART + half * 16 + hops2 * 4 + tz % 4
    code = place + TILES * goal + TILES * TILES * (tile_order + 1)
    wanted = jnp.where(need, rank, 0)[:, :, None] == 1 + jnp.arange(MOST_TILES, dtype=jnp.int32)
    codes = jnp.sum(jnp.where(wanted, code[None, :, None], 0), axis=1)
    counts = rank[:, -1]
    s = jnp.arange(NZ, dtype=jnp.int32)
    ahead = (counts[None, :] > counts[:, None]) | ((counts[None, :] == counts[:, None]) & (s[None, :] < s[:, None]))
    turn = jnp.sum(ahead.astype(jnp.int32), axis=1)
    turns = jnp.sum(jnp.where(turn[None, :] == s[:, None], s[None, :], 0), axis=1)
    return codes, counts, own, ends, turns


def attend(codes, counts, own, ends, turns, qg_ref, kv_hbm, od_ref, *refs):
    parts, (kv_ref, acc, st, sems) = refs[:8], refs[8:]
    load = pltpu.make_async_copy(kv_hbm, kv_ref, sems.at[0])
    load.start()
    acc[...] = jnp.zeros_like(acc)
    load.wait()
    key_at = lax.broadcasted_iota(jnp.int32, (TILE, ROWS), 0)
    lane = lax.broadcasted_iota(jnp.int32, (1, ROWS), 1) & (TILE - 1)

    def stacked(s, start):
        return jnp.concatenate(
            [qg_ref[s, :, start + h * HEAD:start + (h + 1) * HEAD] for h in range(REP)], axis=0)

    def bounds(s):
        q_pos = own[s] * TILE + lane
        low = jnp.zeros_like(q_pos)
        for k in range(4):
            low = jnp.where(q_pos >= ends[k], ends[k], low)
        return q_pos, low

    def rows(c, s, part):
        found = [codes[s, c * CHUNK + j] for j in range(CHUNK)]
        return [kv_ref[f & (TILES - 1), :, part * HEAD:(part + 1) * HEAD] for f in found], found

    def some_tiles(n, carry):
        tiles = [turns[n * TOGETHER + i] for i in range(TOGETHER)]
        q = [stacked(s, 0) for s in tiles]
        g = [stacked(s, WIDE) for s in tiles]
        limits = [bounds(s) for s in tiles]
        chunks = (counts[tiles[0]] + (CHUNK - 1)) // CHUNK

        def scores(c, tops):
            new = []
            for i, s in enumerate(tiles):
                q_pos, low = limits[i]
                keys, found = rows(c, s, 0)
                raw = lax.dot_general(
                    jnp.concatenate(keys, axis=0), q[i], (((1,), (1,)), ((), ())),
                    preferred_element_type=jnp.float32)
                top = tops[i]
                for j, f in enumerate(found):
                    base = (f // (TILES * TILES) - 1) * TILE
                    part = raw[j * TILE:(j + 1) * TILE]
                    part = jnp.where((key_at <= q_pos - base) & (key_at >= low - base), part, NEG)
                    st[i, c, j * TILE:(j + 1) * TILE, :] = part
                    top = jnp.maximum(top, jnp.max(part.reshape(TILE // 8, 8, ROWS), axis=0))
                new.append(top)
            return tuple(new)

        tops = lax.fori_loop(0, chunks, scores, (jnp.full((8, ROWS), NEG, jnp.float32),) * TOGETHER)
        tops = [jnp.max(top, axis=0, keepdims=True) * (SCALE * LOG2E) for top in tops]

        def forward(c, held):
            new = []
            for i, s in enumerate(tiles):
                total, out = held[i]
                prob = jnp.exp2(st[i, c] * (SCALE * LOG2E) - tops[i])
                st[i, c] = prob
                total = total + jnp.sum(prob.reshape(CHUNK * TILE // 8, 8, ROWS), axis=0)
                vals, _ = rows(c, s, 1)
                out = out + lax.dot_general(
                    jnp.concatenate(vals, axis=0), prob.astype(jnp.bfloat16), (((0,), (0,)), ((), ())),
                    preferred_element_type=jnp.float32)
                new.append((total, out))
            return tuple(new)

        start = (jnp.zeros((8, ROWS), jnp.float32), jnp.zeros((HEAD, ROWS), jnp.float32))
        held = lax.fori_loop(0, chunks, forward, (start,) * TOGETHER)
        invs, deltas = [], []
        for i, s in enumerate(tiles):
            total, out = held[i]
            inv = 1.0 / jnp.sum(total, axis=0, keepdims=True)
            out = (out * inv).astype(jnp.bfloat16).astype(jnp.float32)
            invs.append(inv)
            deltas.append(jnp.sum(out * g[i].astype(jnp.float32).T, axis=0, keepdims=True))
            out = out.T.astype(jnp.bfloat16)
            for h in range(REP):
                od_ref[s, :, h * HEAD:(h + 1) * HEAD] = out[h * TILE:(h + 1) * TILE]

        def backward(c, dqs):
            new = []
            for i, s in enumerate(tiles):
                prob = st[i, c] * invs[i]
                keys, found = rows(c, s, 0)
                vals, _ = rows(c, s, 1)
                dprob = lax.dot_general(
                    jnp.concatenate(vals, axis=0), g[i], (((1,), (1,)), ((), ())),
                    preferred_element_type=jnp.float32)
                dscore = (prob * (dprob - deltas[i])).astype(jnp.bfloat16)
                new.append(dqs[i] + lax.dot_general(
                    jnp.concatenate(keys, axis=0), dscore, (((0,), (0,)), ((), ())),
                    preferred_element_type=jnp.float32))
                dk = jnp.dot(dscore, q[i], preferred_element_type=jnp.float32) * SCALE
                dv = jnp.dot(prob.astype(jnp.bfloat16), g[i], preferred_element_type=jnp.float32)
                for j, f in enumerate(found):
                    at = (f // TILES) & (TILES - 1)
                    acc[at, :, :HEAD] = added(acc[at, :, :HEAD], dk[j * TILE:(j + 1) * TILE])
                    acc[at, :, HEAD:] = added(acc[at, :, HEAD:], dv[j * TILE:(j + 1) * TILE])
            return tuple(new)

        dqs = lax.fori_loop(0, chunks, backward, (jnp.zeros((HEAD, ROWS), jnp.float32),) * TOGETHER)
        for s, dq in zip(tiles, dqs):
            dq = (dq * SCALE).T.astype(jnp.bfloat16)
            for h in range(REP):
                od_ref[s, :, WIDE + h * HEAD:WIDE + (h + 1) * HEAD] = dq[h * TILE:(h + 1) * TILE]
        return carry

    lax.fori_loop(0, NZ // TOGETHER, some_tiles, 0)

    stores = [
        pltpu.make_async_copy(acc.at[pl.ds(i * PART, PART)], ref, sems.at[1 + i])
        for i, ref in enumerate(parts)
    ]
    for store in stores:
        store.start()
    for store in stores:
        store.wait()


def attention(codes, counts, own, ends, turns, qg, kv):
    smem = pl.BlockSpec(memory_space=pltpu.SMEM)
    vmem = pl.BlockSpec(memory_space=pltpu.VMEM)
    hbm = pl.BlockSpec(memory_space=pl.ANY)
    part = jax.ShapeDtypeStruct((PART, TILE, 2 * HEAD), jnp.bfloat16)
    return pl.pallas_call(
        attend,
        out_shape=(jax.ShapeDtypeStruct((NZ, TILE, 2 * WIDE), jnp.bfloat16),) + (part,) * 8,
        in_specs=[smem] * 5 + [vmem, hbm],
        out_specs=(vmem,) + (hbm,) * 8,
        scratch_shapes=[
            pltpu.VMEM((TILES, TILE, 2 * HEAD), jnp.bfloat16),
            pltpu.VMEM((TILES, TILE, 2 * HEAD), jnp.bfloat16),
            pltpu.VMEM((TOGETHER, MOST_CHUNKS, CHUNK * TILE, ROWS), jnp.float32),
            pltpu.SemaphoreType.DMA((9,)),
        ],
        compiler_params=pltpu.CompilerParams(vmem_limit_bytes=48 * 1024 * 1024),
        name="attend",
    )(codes, counts, own, ends, turns, qg, kv)


def exchange(blocks, axes):
    return lax.all_to_all(blocks, axes, split_axis=0, concat_axis=0, tiled=True)


def shift(array, axis, by):
    size = lax.axis_size(axis)
    return lax.ppermute(array, axis, [(i, (i + by) % size) for i in range(size)])


def added(*arrays):
    return sum(a.astype(jnp.float32) for a in arrays).astype(jnp.bfloat16)


def summed_at_owner(far, near, beside):
    shape = (2, 4, 4, TILE, 2 * HEAD)
    near = [part.reshape(shape) for part in near]
    other = {hops: shift(far[hops], "core", 1).reshape(shape) for hops in (2, 1, 3, 0)}
    ways = (("x", "y"), ("y", "x"))
    got = ([], [])
    for hops in (2, 1, 3):
        for half, (axis, _) in enumerate(ways):
            got[half].append(shift(added(near[hops][half], other[hops][half]), axis, hops))
    beside, got = lax.optimization_barrier((beside, got))
    parts = []
    for half, (_, axis) in enumerate(ways):
        row = added(near[0][half], other[0][half], *got[half])
        parts.append(added(row[0], *[shift(row[hops], axis, hops) for hops in (2, 1, 3)]))
    return jnp.concatenate(parts), beside


def per_device(queries, keys, values, output_cotangent, tile_order, doc_lengths, read_peer, read_slot):
    order = lax.all_gather(tile_order, ("y", "z", "core"), axis=0, tiled=True)
    lists = plan(order, doc_lengths, read_peer[:, 0], read_slot)

    def by_head(a, b, width):
        both = [v.reshape(TILE, KV_HEADS, width) for v in (a, b)]
        return exchange(jnp.concatenate(both, axis=2).transpose(1, 0, 2), "z")

    def by_token(blocks, width):
        blocks = blocks.transpose(1, 0, 2)
        return [blocks[:, :, i * width:(i + 1) * width].reshape(TILE, KV_HEADS * width) for i in range(2)]

    kv = lax.all_gather(by_head(keys, values, HEAD), ("x", "y", "core"), axis=0, tiled=True)
    kv = kv.reshape(TILES, TILE, 2 * HEAD)
    qg = by_head(queries, output_cotangent, WIDE)
    od, *terms = attention(*lists, qg, kv)
    dkv, od = summed_at_owner(terms[:4], terms[4:], exchange(od, "z"))
    out, dq = by_token(od, WIDE)
    dk, dv = by_token(exchange(dkv, "z"), HEAD)
    return out, dq, dk, dv


def solution(mesh):
    fine = Mesh(mesh.devices.reshape(NY, NZ, NC, NX), AXES)
    rows = P(AXES, None)
    return jax.shard_map(
        per_device,
        mesh=fine,
        in_specs=(rows, rows, rows, rows, P(("y", "z", "core")), P(), P(), P()),
        out_specs=(rows, rows, rows, rows),
        check_vma=False,
    )
```

```python
import jax
import jax.numpy as jnp
from jax import lax
from jax.experimental import pallas as pl
from jax.experimental.pallas import tpu as pltpu
from jax.sharding import Mesh, PartitionSpec as P

HEAD = 128
TILE = 64
SLOTS = 4
KV_HEADS = 8
REP = 4
NX, NY, NZ, NC = 4, 4, 8, 2
GROUPS = NY * NZ * NC
TILES = GROUPS * SLOTS
READS = 64
CHUNK = 12
MOST_TILES = 72
MOST_CHUNKS = MOST_TILES // CHUNK
ROWS = REP * TILE
WIDE = REP * HEAD
PART = TILES // 8
TOGETHER = 2
SCALE = HEAD ** -0.5
LOG2E = 1.4426950408889634
AXES = ("y", "z", "core", "x")
NEG = -1e30


def plan(tile_order, doc_lengths, read_peer, read_slot):
    x, y, core = lax.axis_index("x"), lax.axis_index("y"), lax.axis_index("core")
    ends = jnp.cumsum(doc_lengths, dtype=jnp.int32)

    def mine(table):
        table = table.reshape(NY, NZ, NC, READS)
        table = lax.dynamic_index_in_dim(table, y, 0, keepdims=False)
        return lax.dynamic_index_in_dim(table, core, 1, keepdims=False)

    peers, bases = mine(read_peer), mine(read_slot)
    group = (y * NZ + jnp.arange(NZ, dtype=jnp.int32)) * NC + core
    all_groups = jnp.arange(GROUPS, dtype=jnp.int32)
    same = peers[:, :, None] == all_groups[None, None, :]
    count = jnp.sum(same.astype(jnp.int32), axis=1)
    entry = jnp.arange(READS, dtype=jnp.int32)
    first = jnp.min(jnp.where(same, (entry[None, :] * SLOTS + bases)[:, :, None], READS * SLOTS), axis=1)
    slot = jnp.arange(SLOTS, dtype=jnp.int32)
    listed = ((slot[None, None, :] - first[:, :, None]) & (SLOTS - 1)) < count[:, :, None]
    listed = listed | (all_groups[None, :] == group[:, None])[:, :, None]
    listed = listed.reshape(NZ, TILES)
    order = tile_order.reshape(NY, NZ, NC, SLOTS)
    own = lax.dynamic_index_in_dim(order, y, 0, keepdims=False)
    own = lax.dynamic_index_in_dim(own, core, 1, keepdims=False)
    own = lax.dynamic_index_in_dim(own, x, 1, keepdims=False)
    start = jnp.max(jnp.where(ends[None, :] <= own[:, None] * TILE, ends[None, :], 0), axis=1)
    need = (
        listed
        & (tile_order[None, :] <= own[:, None])
        & (tile_order[None, :] * TILE + (TILE - 1) >= start[:, None])
    )
    rank = jnp.cumsum(need.astype(jnp.int32), axis=1)
    t = jnp.arange(TILES, dtype=jnp.int32)
    tx, tc, tz, ty = t % 4, (t // 4) % 2, (t // 8) % 8, t // 64
    place = ((tx * NY + ty) * NC + tc) * NZ + tz
    dx, dy, half = (tx - x) & 3, (ty - y) & 3, tz // 4
    hops, hops2 = jnp.where(half == 0, dx, dy), jnp.where(half == 0, dy, dx)
    goal = ((1 - (tc ^ core)) * 4 + hops) * PART + half * 16 + hops2 * 4 + tz % 4
    code = place + TILES * goal + TILES * TILES * (tile_order + 1)
    wanted = jnp.where(need, rank, 0)[:, :, None] == 1 + jnp.arange(MOST_TILES, dtype=jnp.int32)
    codes = jnp.sum(jnp.where(wanted, code[None, :, None], 0), axis=1)
    counts = rank[:, -1]
    s = jnp.arange(NZ, dtype=jnp.int32)
    ahead = (counts[None, :] > counts[:, None]) | ((counts[None, :] == counts[:, None]) & (s[None, :] < s[:, None]))
    turn = jnp.sum(ahead.astype(jnp.int32), axis=1)
    turns = jnp.sum(jnp.where(turn[None, :] == s[:, None], s[None, :], 0), axis=1)
    return codes, counts, own, ends, turns


def attend(codes, counts, own, ends, turns, qg_ref, kv_hbm, od_ref, *refs):
    parts, (kv_ref, acc, st, sems) = refs[:8], refs[8:]
    load = pltpu.make_async_copy(kv_hbm, kv_ref, sems.at[0])
    load.start()
    acc[...] = jnp.zeros_like(acc)
    load.wait()
    key_at = lax.broadcasted_iota(jnp.int32, (TILE, ROWS), 0).astype(jnp.float32)
    lane = lax.broadcasted_iota(jnp.int32, (1, ROWS), 1) & (TILE - 1)

    def stacked(s, start):
        return jnp.concatenate(
            [qg_ref[s, :, start + h * HEAD:start + (h + 1) * HEAD] for h in range(REP)], axis=0)

    def bounds(s):
        q_pos = own[s] * TILE + lane
        low = jnp.zeros_like(q_pos)
        for k in range(4):
            low = jnp.where(q_pos >= ends[k], ends[k], low)
        return q_pos, low

    def rows(c, s, part):
        found = [codes[s, c * CHUNK + j] for j in range(CHUNK)]
        return [kv_ref[f & (TILES - 1), :, part * HEAD:(part + 1) * HEAD] for f in found], found

    def some_tiles(n, carry):
        tiles = [turns[n * TOGETHER + i] for i in range(TOGETHER)]
        q = [stacked(s, 0) for s in tiles]
        g = [stacked(s, WIDE) for s in tiles]
        limits = [bounds(s) for s in tiles]
        chunks = (counts[tiles[0]] + (CHUNK - 1)) // CHUNK

        def scores(c, tops):
            new = []
            for i, s in enumerate(tiles):
                q_pos, low = limits[i]
                keys, found = rows(c, s, 0)
                raw = lax.dot_general(
                    jnp.concatenate(keys, axis=0), q[i], (((1,), (1,)), ((), ())),
                    preferred_element_type=jnp.float32)
                top = tops[i]
                for j, f in enumerate(found):
                    base = (f // (TILES * TILES) - 1) * TILE
                    part = raw[j * TILE:(j + 1) * TILE]
                    part = jnp.where((key_at <= (q_pos - base).astype(jnp.float32)) & (key_at >= (low - base).astype(jnp.float32)), part, NEG)
                    st[i, c, j * TILE:(j + 1) * TILE, :] = part
                    top = jnp.maximum(top, jnp.max(part.reshape(TILE // 8, 8, ROWS), axis=0))
                new.append(top)
            return tuple(new)

        tops = lax.fori_loop(0, chunks, scores, (jnp.full((8, ROWS), NEG, jnp.float32),) * TOGETHER)
        tops = [jnp.max(top, axis=0, keepdims=True) * (SCALE * LOG2E) for top in tops]

        def forward(c, held):
            new = []
            for i, s in enumerate(tiles):
                total, out = held[i]
                prob = jnp.exp2(st[i, c] * (SCALE * LOG2E) - tops[i])
                st[i, c] = prob
                total = total + jnp.sum(prob.reshape(CHUNK * TILE // 8, 8, ROWS), axis=0)
                vals, _ = rows(c, s, 1)
                out = out + lax.dot_general(
                    jnp.concatenate(vals, axis=0), prob.astype(jnp.bfloat16), (((0,), (0,)), ((), ())),
                    preferred_element_type=jnp.float32)
                new.append((total, out))
            return tuple(new)

        start = (jnp.zeros((8, ROWS), jnp.float32), jnp.zeros((HEAD, ROWS), jnp.float32))
        held = lax.fori_loop(0, chunks, forward, (start,) * TOGETHER)
        invs, deltas = [], []
        for i, s in enumerate(tiles):
            total, out = held[i]
            inv = 1.0 / jnp.sum(total, axis=0, keepdims=True)
            out = (out * inv).astype(jnp.bfloat16).astype(jnp.float32)
            invs.append(inv)
            deltas.append(jnp.sum(out * g[i].astype(jnp.float32).T, axis=0, keepdims=True))
            out = out.T.astype(jnp.bfloat16)
            for h in range(REP):
                od_ref[s, :, h * HEAD:(h + 1) * HEAD] = out[h * TILE:(h + 1) * TILE]

        def backward(c, dqs):
            new = []
            for i, s in enumerate(tiles):
                prob = st[i, c] * invs[i]
                keys, found = rows(c, s, 0)
                vals, _ = rows(c, s, 1)
                dprob = lax.dot_general(
                    jnp.concatenate(vals, axis=0), g[i], (((1,), (1,)), ((), ())),
                    preferred_element_type=jnp.float32)
                dscore = (prob * (dprob - deltas[i])).astype(jnp.bfloat16)
                new.append(dqs[i] + lax.dot_general(
                    jnp.concatenate(keys, axis=0), dscore, (((0,), (0,)), ((), ())),
                    preferred_element_type=jnp.float32))
                dk = jnp.dot(dscore, q[i], preferred_element_type=jnp.float32) * SCALE
                dv = jnp.dot(prob.astype(jnp.bfloat16), g[i], preferred_element_type=jnp.float32)
                for j, f in enumerate(found):
                    at = (f // TILES) & (TILES - 1)
                    acc[at, :, :HEAD] = added(acc[at, :, :HEAD], dk[j * TILE:(j + 1) * TILE])
                    acc[at, :, HEAD:] = added(acc[at, :, HEAD:], dv[j * TILE:(j + 1) * TILE])
            return tuple(new)

        dqs = lax.fori_loop(0, chunks, backward, (jnp.zeros((HEAD, ROWS), jnp.float32),) * TOGETHER)
        for s, dq in zip(tiles, dqs):
            dq = (dq * SCALE).T.astype(jnp.bfloat16)
            for h in range(REP):
                od_ref[s, :, WIDE + h * HEAD:WIDE + (h + 1) * HEAD] = dq[h * TILE:(h + 1) * TILE]
        return carry

    lax.fori_loop(0, NZ // TOGETHER, some_tiles, 0)

    stores = [
        pltpu.make_async_copy(acc.at[pl.ds(i * PART, PART)], ref, sems.at[1 + i])
        for i, ref in enumerate(parts)
    ]
    for store in stores:
        store.start()
    for store in stores:
        store.wait()


def attention(codes, counts, own, ends, turns, qg, kv):
    smem = pl.BlockSpec(memory_space=pltpu.SMEM)
    vmem = pl.BlockSpec(memory_space=pltpu.VMEM)
    hbm = pl.BlockSpec(memory_space=pl.ANY)
    part = jax.ShapeDtypeStruct((PART, TILE, 2 * HEAD), jnp.bfloat16)
    return pl.pallas_call(
        attend,
        out_shape=(jax.ShapeDtypeStruct((NZ, TILE, 2 * WIDE), jnp.bfloat16),) + (part,) * 8,
        in_specs=[smem] * 5 + [vmem, hbm],
        out_specs=(vmem,) + (hbm,) * 8,
        scratch_shapes=[
            pltpu.VMEM((TILES, TILE, 2 * HEAD), jnp.bfloat16),
            pltpu.VMEM((TILES, TILE, 2 * HEAD), jnp.bfloat16),
            pltpu.VMEM((TOGETHER, MOST_CHUNKS, CHUNK * TILE, ROWS), jnp.float32),
            pltpu.SemaphoreType.DMA((9,)),
        ],
        compiler_params=pltpu.CompilerParams(vmem_limit_bytes=48 * 1024 * 1024),
        name="attend",
    )(codes, counts, own, ends, turns, qg, kv)


def exchange(blocks, axes):
    return lax.all_to_all(blocks, axes, split_axis=0, concat_axis=0, tiled=True)


def shift(array, axis, by):
    size = lax.axis_size(axis)
    return lax.ppermute(array, axis, [(i, (i + by) % size) for i in range(size)])


def added(*arrays):
    return sum(a.astype(jnp.float32) for a in arrays).astype(jnp.bfloat16)


def summed_at_owner(far, near, beside):
    shape = (2, 4, 4, TILE, 2 * HEAD)
    near = [part.reshape(shape) for part in near]
    other = {hops: shift(far[hops], "core", 1).reshape(shape) for hops in (2, 1, 3, 0)}
    ways = (("x", "y"), ("y", "x"))
    got = ([], [])
    for hops in (2, 1, 3):
        for half, (axis, _) in enumerate(ways):
            got[half].append(shift(added(near[hops][half], other[hops][half]), axis, hops))
    beside, got = lax.optimization_barrier((beside, got))
    parts = []
    for half, (_, axis) in enumerate(ways):
        row = added(near[0][half], other[0][half], *got[half])
        parts.append(added(row[0], *[shift(row[hops], axis, hops) for hops in (2, 1, 3)]))
    return jnp.concatenate(parts), beside


def per_device(queries, keys, values, output_cotangent, tile_order, doc_lengths, read_peer, read_slot):
    order = lax.all_gather(tile_order, ("y", "z", "core"), axis=0, tiled=True)
    lists = plan(order, doc_lengths, read_peer[:, 0], read_slot)

    def by_head(a, b, width):
        both = [v.reshape(TILE, KV_HEADS, width) for v in (a, b)]
        return exchange(jnp.concatenate(both, axis=2).transpose(1, 0, 2), "z")

    def by_token(blocks, width):
        blocks = blocks.transpose(1, 0, 2)
        return [blocks[:, :, i * width:(i + 1) * width].reshape(TILE, KV_HEADS * width) for i in range(2)]

    cuts = [slice(h * HEAD, (h + 1) * HEAD) for h in range(KV_HEADS)]
    block = jnp.stack([jnp.concatenate([keys[:, cut], values[:, cut]], axis=1) for cut in cuts])
    kv = lax.all_gather(exchange(block, "z"), ("x", "y", "core"), axis=0, tiled=True)
    kv = kv.reshape(TILES, TILE, 2 * HEAD)
    qg = by_head(queries, output_cotangent, WIDE)
    od, *terms = attention(*lists, qg, kv)
    dkv, od = summed_at_owner(terms[:4], terms[4:], exchange(od, "z"))
    out, dq = by_token(od, WIDE)
    dk, dv = by_token(exchange(dkv, "z"), HEAD)
    return out, dq, dk, dv


def solution(mesh):
    fine = Mesh(mesh.devices.reshape(NY, NZ, NC, NX), AXES)
    rows = P(AXES, None)
    return jax.shard_map(
        per_device,
        mesh=fine,
        in_specs=(rows, rows, rows, rows, P(("y", "z", "core")), P(), P(), P()),
        out_specs=(rows, rows, rows, rows),
        check_vma=False,
    )
```

```python
import jax
import jax.numpy as jnp
from jax import lax
from jax.experimental import pallas as pl
from jax.experimental.pallas import tpu as pltpu
from jax.sharding import Mesh, PartitionSpec as P

HEAD = 128
TILE = 64
SLOTS = 4
KV_HEADS = 8
REP = 4
NX, NY, NZ, NC = 4, 4, 8, 2
GROUPS = NY * NZ * NC
TILES = GROUPS * SLOTS
READS = 64
CHUNK = 12
MOST_TILES = 72
MOST_CHUNKS = MOST_TILES // CHUNK
ROWS = REP * TILE
WIDE = REP * HEAD
PART = TILES // 8
TOGETHER = 2
SCALE = HEAD ** -0.5
LOG2E = 1.4426950408889634
AXES = ("y", "z", "core", "x")
NEG = -1e30


def plan(tile_order, doc_lengths, read_peer, read_slot):
    x, y, core = lax.axis_index("x"), lax.axis_index("y"), lax.axis_index("core")
    ends = jnp.cumsum(doc_lengths, dtype=jnp.int32)

    def mine(table):
        table = table.reshape(NY, NZ, NC, READS)
        table = lax.dynamic_index_in_dim(table, y, 0, keepdims=False)
        return lax.dynamic_index_in_dim(table, core, 1, keepdims=False)

    peers, bases = mine(read_peer), mine(read_slot)
    group = (y * NZ + jnp.arange(NZ, dtype=jnp.int32)) * NC + core
    all_groups = jnp.arange(GROUPS, dtype=jnp.int32)
    same = peers[:, :, None] == all_groups[None, None, :]
    count = jnp.sum(same.astype(jnp.int32), axis=1)
    entry = jnp.arange(READS, dtype=jnp.int32)
    first = jnp.min(jnp.where(same, (entry[None, :] * SLOTS + bases)[:, :, None], READS * SLOTS), axis=1)
    slot = jnp.arange(SLOTS, dtype=jnp.int32)
    listed = ((slot[None, None, :] - first[:, :, None]) & (SLOTS - 1)) < count[:, :, None]
    listed = listed | (all_groups[None, :] == group[:, None])[:, :, None]
    listed = listed.reshape(NZ, TILES)
    order = tile_order.reshape(NY, NZ, NC, SLOTS)
    own = lax.dynamic_index_in_dim(order, y, 0, keepdims=False)
    own = lax.dynamic_index_in_dim(own, core, 1, keepdims=False)
    own = lax.dynamic_index_in_dim(own, x, 1, keepdims=False)
    start = jnp.max(jnp.where(ends[None, :] <= own[:, None] * TILE, ends[None, :], 0), axis=1)
    need = (
        listed
        & (tile_order[None, :] <= own[:, None])
        & (tile_order[None, :] * TILE + (TILE - 1) >= start[:, None])
    )
    rank = jnp.cumsum(need.astype(jnp.int32), axis=1)
    t = jnp.arange(TILES, dtype=jnp.int32)
    tx, tc, tz, ty = t % 4, (t // 4) % 2, (t // 8) % 8, t // 64
    place = ((tx * NY + ty) * NC + tc) * NZ + tz
    dx, dy, half = (tx - x) & 3, (ty - y) & 3, tz // 4
    hops, hops2 = jnp.where(half == 0, dx, dy), jnp.where(half == 0, dy, dx)
    goal = ((1 - (tc ^ core)) * 4 + hops) * PART + half * 16 + hops2 * 4 + tz % 4
    code = place + TILES * goal + TILES * TILES * (tile_order + 1)
    wanted = jnp.where(need, rank, 0)[:, :, None] == 1 + jnp.arange(MOST_TILES, dtype=jnp.int32)
    codes = jnp.sum(jnp.where(wanted, code[None, :, None], 0), axis=1)
    counts = rank[:, -1]
    s = jnp.arange(NZ, dtype=jnp.int32)
    ahead = (counts[None, :] > counts[:, None]) | ((counts[None, :] == counts[:, None]) & (s[None, :] < s[:, None]))
    turn = jnp.sum(ahead.astype(jnp.int32), axis=1)
    turns = jnp.sum(jnp.where(turn[None, :] == s[:, None], s[None, :], 0), axis=1)
    return codes, counts, own, ends, turns


def attend(codes, counts, own, ends, turns, qg_ref, kv_hbm, od_ref, *refs):
    parts, (kv_ref, acc, st, sems) = refs[:8], refs[8:]
    loads = [
        pltpu.make_async_copy(kv_hbm.at[:, :, cut], kv_ref.at[:, :, cut], sems.at[i])
        for i, cut in ((0, pl.ds(0, HEAD)), (9, pl.ds(HEAD, HEAD)))]
    for load in loads:
        load.start()
    acc[...] = jnp.zeros_like(acc)
    loads[0].wait()
    key_at = lax.broadcasted_iota(jnp.int32, (TILE, ROWS), 0).astype(jnp.float32)
    lane = lax.broadcasted_iota(jnp.int32, (1, ROWS), 1) & (TILE - 1)

    def stacked(s, start):
        return jnp.concatenate(
            [qg_ref[s, :, start + h * HEAD:start + (h + 1) * HEAD] for h in range(REP)], axis=0)

    def bounds(s):
        q_pos = own[s] * TILE + lane
        low = jnp.zeros_like(q_pos)
        for k in range(4):
            low = jnp.where(q_pos >= ends[k], ends[k], low)
        return q_pos, low

    def rows(c, s, part):
        found = [codes[s, c * CHUNK + j] for j in range(CHUNK)]
        return [kv_ref[f & (TILES - 1), :, part * HEAD:(part + 1) * HEAD] for f in found], found

    def some_tiles(n, carry):
        tiles = [turns[n * TOGETHER + i] for i in range(TOGETHER)]
        q = [stacked(s, 0) for s in tiles]
        g = [stacked(s, WIDE) for s in tiles]
        limits = [bounds(s) for s in tiles]
        chunks = (counts[tiles[0]] + (CHUNK - 1)) // CHUNK

        def scores(c, tops):
            new = []
            for i, s in enumerate(tiles):
                q_pos, low = limits[i]
                keys, found = rows(c, s, 0)
                raw = lax.dot_general(
                    jnp.concatenate(keys, axis=0), q[i], (((1,), (1,)), ((), ())),
                    preferred_element_type=jnp.float32)
                top = tops[i]
                for j, f in enumerate(found):
                    base = (f // (TILES * TILES) - 1) * TILE
                    part = raw[j * TILE:(j + 1) * TILE]
                    part = jnp.where((key_at <= (q_pos - base).astype(jnp.float32)) & (key_at >= (low - base).astype(jnp.float32)), part, NEG)
                    st[i, c, j * TILE:(j + 1) * TILE, :] = part
                    top = jnp.maximum(top, jnp.max(part.reshape(TILE // 8, 8, ROWS), axis=0))
                new.append(top)
            return tuple(new)

        tops = lax.fori_loop(0, chunks, scores, (jnp.full((8, ROWS), NEG, jnp.float32),) * TOGETHER)

        @pl.when(n == 0)
        def _():
            loads[1].wait()

        tops = [jnp.max(top, axis=0, keepdims=True) * (SCALE * LOG2E) for top in tops]

        def forward(c, held):
            new = []
            for i, s in enumerate(tiles):
                total, out = held[i]
                prob = jnp.exp2(st[i, c] * (SCALE * LOG2E) - tops[i])
                st[i, c] = prob
                total = total + jnp.sum(prob.reshape(CHUNK * TILE // 8, 8, ROWS), axis=0)
                vals, _ = rows(c, s, 1)
                out = out + lax.dot_general(
                    jnp.concatenate(vals, axis=0), prob.astype(jnp.bfloat16), (((0,), (0,)), ((), ())),
                    preferred_element_type=jnp.float32)
                new.append((total, out))
            return tuple(new)

        start = (jnp.zeros((8, ROWS), jnp.float32), jnp.zeros((HEAD, ROWS), jnp.float32))
        held = lax.fori_loop(0, chunks, forward, (start,) * TOGETHER)
        invs, deltas = [], []
        for i, s in enumerate(tiles):
            total, out = held[i]
            inv = 1.0 / jnp.sum(total, axis=0, keepdims=True)
            out = (out * inv).astype(jnp.bfloat16).astype(jnp.float32)
            invs.append(inv)
            deltas.append(jnp.sum(out * g[i].astype(jnp.float32).T, axis=0, keepdims=True))
            out = out.T.astype(jnp.bfloat16)
            for h in range(REP):
                od_ref[s, :, h * HEAD:(h + 1) * HEAD] = out[h * TILE:(h + 1) * TILE]

        def backward(c, dqs):
            new = []
            for i, s in enumerate(tiles):
                prob = st[i, c] * invs[i]
                keys, found = rows(c, s, 0)
                vals, _ = rows(c, s, 1)
                dprob = lax.dot_general(
                    jnp.concatenate(vals, axis=0), g[i], (((1,), (1,)), ((), ())),
                    preferred_element_type=jnp.float32)
                dscore = (prob * (dprob - deltas[i])).astype(jnp.bfloat16)
                new.append(dqs[i] + lax.dot_general(
                    jnp.concatenate(keys, axis=0), dscore, (((0,), (0,)), ((), ())),
                    preferred_element_type=jnp.float32))
                dk = jnp.dot(dscore, q[i], preferred_element_type=jnp.float32) * SCALE
                dv = jnp.dot(prob.astype(jnp.bfloat16), g[i], preferred_element_type=jnp.float32)
                for j, f in enumerate(found):
                    at = (f // TILES) & (TILES - 1)
                    acc[at, :, :HEAD] = added(acc[at, :, :HEAD], dk[j * TILE:(j + 1) * TILE])
                    acc[at, :, HEAD:] = added(acc[at, :, HEAD:], dv[j * TILE:(j + 1) * TILE])
            return tuple(new)

        dqs = lax.fori_loop(0, chunks, backward, (jnp.zeros((HEAD, ROWS), jnp.float32),) * TOGETHER)
        for s, dq in zip(tiles, dqs):
            dq = (dq * SCALE).T.astype(jnp.bfloat16)
            for h in range(REP):
                od_ref[s, :, WIDE + h * HEAD:WIDE + (h + 1) * HEAD] = dq[h * TILE:(h + 1) * TILE]
        return carry

    lax.fori_loop(0, NZ // TOGETHER, some_tiles, 0)

    stores = [
        pltpu.make_async_copy(acc.at[pl.ds(i * PART, PART)], ref, sems.at[1 + i])
        for i, ref in enumerate(parts)
    ]
    for store in stores:
        store.start()
    for store in stores:
        store.wait()


def attention(codes, counts, own, ends, turns, qg, kv):
    smem = pl.BlockSpec(memory_space=pltpu.SMEM)
    vmem = pl.BlockSpec(memory_space=pltpu.VMEM)
    hbm = pl.BlockSpec(memory_space=pl.ANY)
    part = jax.ShapeDtypeStruct((PART, TILE, 2 * HEAD), jnp.bfloat16)
    return pl.pallas_call(
        attend,
        out_shape=(jax.ShapeDtypeStruct((NZ, TILE, 2 * WIDE), jnp.bfloat16),) + (part,) * 8,
        in_specs=[smem] * 5 + [vmem, hbm],
        out_specs=(vmem,) + (hbm,) * 8,
        scratch_shapes=[
            pltpu.VMEM((TILES, TILE, 2 * HEAD), jnp.bfloat16),
            pltpu.VMEM((TILES, TILE, 2 * HEAD), jnp.bfloat16),
            pltpu.VMEM((TOGETHER, MOST_CHUNKS, CHUNK * TILE, ROWS), jnp.float32),
            pltpu.SemaphoreType.DMA((10,)),
        ],
        compiler_params=pltpu.CompilerParams(vmem_limit_bytes=48 * 1024 * 1024),
        name="attend",
    )(codes, counts, own, ends, turns, qg, kv)


def exchange(blocks, axes):
    return lax.all_to_all(blocks, axes, split_axis=0, concat_axis=0, tiled=True)


def shift(array, axis, by):
    size = lax.axis_size(axis)
    return lax.ppermute(array, axis, [(i, (i + by) % size) for i in range(size)])


def added(*arrays):
    return sum(a.astype(jnp.float32) for a in arrays).astype(jnp.bfloat16)


def summed_at_owner(far, near, beside):
    shape = (2, 4, 4, TILE, 2 * HEAD)
    near = [part.reshape(shape) for part in near]
    other = {hops: shift(far[hops], "core", 1).reshape(shape) for hops in (2, 1, 3, 0)}
    ways = (("x", "y"), ("y", "x"))
    got = ([], [])
    for hops in (2, 1, 3):
        for half, (axis, _) in enumerate(ways):
            got[half].append(shift(added(near[hops][half], other[hops][half]), axis, hops))
    beside, got = lax.optimization_barrier((beside, got))
    parts = []
    for half, (_, axis) in enumerate(ways):
        row = added(near[0][half], other[0][half], *got[half])
        parts.append(added(row[0], *[shift(row[hops], axis, hops) for hops in (2, 1, 3)]))
    return jnp.concatenate(parts), beside


def per_device(queries, keys, values, output_cotangent, tile_order, doc_lengths, read_peer, read_slot):
    order = lax.all_gather(tile_order, ("y", "z", "core"), axis=0, tiled=True)
    lists = plan(order, doc_lengths, read_peer[:, 0], read_slot)

    def by_head(a, b, width):
        both = [v.reshape(TILE, KV_HEADS, width) for v in (a, b)]
        return exchange(jnp.concatenate(both, axis=2).transpose(1, 0, 2), "z")

    def by_token(blocks, width):
        blocks = blocks.transpose(1, 0, 2)
        return [blocks[:, :, i * width:(i + 1) * width].reshape(TILE, KV_HEADS * width) for i in range(2)]

    cuts = [slice(h * HEAD, (h + 1) * HEAD) for h in range(KV_HEADS)]
    block = jnp.stack([jnp.concatenate([keys[:, cut], values[:, cut]], axis=1) for cut in cuts])
    kv = lax.all_gather(exchange(block, "z"), ("x", "y", "core"), axis=0, tiled=True)
    kv = kv.reshape(TILES, TILE, 2 * HEAD)
    qg = by_head(queries, output_cotangent, WIDE)
    od, *terms = attention(*lists, qg, kv)
    dkv, od = summed_at_owner(terms[:4], terms[4:], exchange(od, "z"))
    out, dq = by_token(od, WIDE)
    dk, dv = by_token(exchange(dkv, "z"), HEAD)
    return out, dq, dk, dv


def solution(mesh):
    fine = Mesh(mesh.devices.reshape(NY, NZ, NC, NX), AXES)
    rows = P(AXES, None)
    return jax.shard_map(
        per_device,
        mesh=fine,
        in_specs=(rows, rows, rows, rows, P(("y", "z", "core")), P(), P(), P()),
        out_specs=(rows, rows, rows, rows),
        check_vma=False,
    )
```
